32 devices in a mesh: groups: 2 (over x), seq: 16 (over z, y, core).
Axes of the slice: x: 2, y: 2, z: 4, core: 2. Of those that a mesh axis runs over, the one named last changes fastest.
Arguments:
- queries: bfloat16 [32, 4, 8192], P(('groups', 'seq')), parts along dimension 0, may hold values from -256 to 256
- base_cache: bfloat16 [16384, 2048], P(('groups', 'seq')), parts along dimension 0, may hold values from -8 to 8
- page_pool: bfloat16 [64, 128, 2048], P(('groups', 'seq')), parts along dimension 0, may hold values from -6 to 6
- new_cache: bfloat16 [32, 4, 2048], P(('groups', 'seq')), parts along dimension 0, may hold values from -12 to 12
- page_table: int32 [32, 2], P('groups'), parts along dimension 0, may hold values from 0 to 31, as said below
- offsets: int32 [32], P('groups'), parts along dimension 0, may hold values from 1024 to 8192
- lengths: int32 [32], P('groups'), parts along dimension 0, may hold values from 1 to 256
Outputs:
- attended: bfloat16 [32, 4, 8192], P(('groups', 'seq')), parts along dimension 0
The draws below stay inside these ranges and needn't reach their ends.
There are 2 independent parts, one for each index of `groups`. The reference program is written for one: setup_inputs(seed, part) draws one part's arguments, and reference() takes and returns one part's arrays. A program takes and returns all parts, laid end to end along the dimension named above; each array names one. Nothing has to cross between parts.
Inputs may be any that keep to these rules, and one draw needn't show every extreme that they name: `page_table`: each of the 32 pool pages is named by exactly one entry.
All inputs are finite; a program needn't handle non-finite values.
Results may differ from the reference program's by a relative error of at most 0.0075.
Values may be sent and summed in bfloat16 or wider, within the bound.
A program may use at most 128 MiB of HBM per device.

```python
import jax
import jax.numpy as jnp
from jax import lax

QH = 64
KVH = 8
HD = 128
STEPS = 4
PAGE = 128
PMAX = 2
ROWS = 16
BASE = 8192
CTX = 256


def prefix_rows(key):
    raw_rows = jax.random.normal(jax.random.fold_in(key, 101), (BASE, KVH * 2 * HD), jnp.float32)
    return jnp.clip(raw_rows, -6.0, 6.0)


def draw_base_cache(key, part):
    raw_rows = prefix_rows(key)
    return raw_rows.astype(jnp.bfloat16)


def draw_queries(key, part):
    key = jax.random.fold_in(key, 13)
    drawn_draw = jnp.clip(jax.random.normal(key, (ROWS, STEPS, QH * HD), jnp.float32), -6.0, 6.0)
    return drawn_draw.astype(jnp.bfloat16)


def draw_page_table(key, part):
    key = jax.random.fold_in(key, 21)
    return jax.random.permutation(key, ROWS * PMAX).astype(jnp.int32).reshape(ROWS, PMAX)


def ends_forced(key, lowest, highest):
    first_key, second_key, third_key = jax.random.split(key, 3)
    values = jax.random.randint(first_key, (ROWS,), lowest, highest + 1, dtype=jnp.int32)
    top_row = jax.random.randint(second_key, (), 0, ROWS, dtype=jnp.int32)
    bottom = (top_row + 1 + jax.random.randint(third_key, (), 0, ROWS - 1, dtype=jnp.int32)) % ROWS
    return values.at[top_row].set(highest).at[bottom].set(lowest)


def draw_offsets(key, part):
    key = jax.random.fold_in(key, 31)
    return ends_forced(key, BASE // 8, BASE)


def draw_lengths(key, part):
    key = jax.random.fold_in(key, 41)
    return ends_forced(key, 1, CTX)


def level_of(key, shape, shards, smallest, largest):
    level = 1.0
    for position, blocks in shards:
        draws = jax.random.uniform(jax.random.fold_in(jax.random.fold_in(key, 6), position), (blocks,), jnp.float32, smallest / len(shards), largest / len(shards))
        level = level * jnp.repeat(jnp.exp(draws), shape[position] // blocks).reshape((-1,) + (1,) * (len(shape) - 1 - position))
    return level


def noise(key, extent, width, limit, shards=(), kind=jnp.bfloat16):
    array = jax.random.normal(key, extent, jnp.float32) * width
    if len(shards) > 0:
        array = level_of(key, extent, shards, -0.22, 0.18) * array
    return jnp.clip(array, min=-limit, max=limit).astype(kind)


def setup_inputs(seed: int = 0, part: int = 0) -> dict:
    streams_of = jax.random.split(jax.random.key(seed), 8)
    own_keys = jax.random.split(jax.random.fold_in(streams_of[7], part), 8)
    queries = draw_queries(jax.random.fold_in(jax.random.fold_in(streams_of[7], part), 71), part)
    base_cache = draw_base_cache(jax.random.fold_in(jax.random.fold_in(streams_of[7], part), 71), part)
    page_pool = noise(own_keys[2], (ROWS * PMAX, PAGE, KVH * 2 * HD), 1.0, 6.0, ((0, 16),))
    new_cache = noise(own_keys[3], (ROWS, STEPS, KVH * 2 * HD), 2.0, 12.0, ((0, 16),))
    page_table = draw_page_table(jax.random.fold_in(jax.random.fold_in(streams_of[7], part), 71), part)
    offsets = draw_offsets(jax.random.fold_in(jax.random.fold_in(streams_of[7], part), 71), part)
    lengths = draw_lengths(jax.random.fold_in(jax.random.fold_in(streams_of[7], part), 71), part)
    return {"queries": queries, "base_cache": base_cache, "page_pool": page_pool, "new_cache": new_cache, "page_table": page_table, "offsets": offsets, "lengths": lengths}


far_below = -1.0e30
strict_setting = lax.Precision.HIGHEST


def rounded(weights):
    return lax.optimization_barrier(weights.astype(jnp.bfloat16)).astype(jnp.float32)


def reference(queries, base_cache, page_pool, new_cache, page_table, offsets, lengths):
    row_count = queries.shape[0]
    group_size = QH // KVH
    score_scale = HD ** -0.5
    private = page_pool[page_table].reshape(row_count, PMAX * PAGE, KVH * 2 * HD)
    base_live = jnp.arange(BASE, dtype=jnp.int32)[None, :] < offsets[:, None]
    page_live = jnp.arange(PMAX * PAGE, dtype=jnp.int32)[None, :] < lengths[:, None]
    step_ids = jnp.arange(STEPS, dtype=jnp.int32)
    new_live = step_ids[None, :] <= step_ids[:, None]

    def one_head(head_id):
        head_width = group_size * HD
        query_block = lax.dynamic_slice_in_dim(queries, head_id * head_width, head_width, 2)
        query_block = query_block.astype(jnp.float32).reshape(row_count, STEPS, group_size, HD)

        def columns_of(source, offset):
            return lax.dynamic_slice_in_dim(source, head_id * 2 * HD + offset, HD, source.ndim - 1).astype(jnp.float32)

        base_keys, base_values = columns_of(base_cache, 0), columns_of(base_cache, HD)
        page_keys, page_values = columns_of(private, 0), columns_of(private, HD)
        new_keys, new_values = columns_of(new_cache, 0), columns_of(new_cache, HD)
        base_scores = jnp.einsum('bsgd,td->bsgt', query_block, base_keys, precision=strict_setting) * score_scale
        page_scores = jnp.einsum('bsgd,bcd->bsgc', query_block, page_keys, precision=strict_setting) * score_scale
        new_scores = jnp.einsum('bsgd,bud->bsgu', query_block, new_keys, precision=strict_setting) * score_scale
        base_mask = base_live[:, None, None, :]
        page_mask = page_live[:, None, None, :]
        new_mask = new_live[None, :, None, :]
        base_scores = jnp.where(base_mask, base_scores, far_below)
        page_scores = jnp.where(page_mask, page_scores, far_below)
        new_scores = jnp.where(new_mask, new_scores, far_below)
        row_top = jnp.maximum(jnp.maximum(jnp.max(base_scores, axis=3), jnp.max(page_scores, axis=3)), jnp.max(new_scores, axis=3))
        prefix_weights = jnp.where(base_mask, jnp.exp(base_scores - row_top[..., None]), 0.0)
        page_weights = jnp.where(page_mask, jnp.exp(page_scores - row_top[..., None]), 0.0)
        new_weights = jnp.where(new_mask, jnp.exp(new_scores - row_top[..., None]), 0.0)
        numerator = jnp.einsum('bsgt,td->bsgd', rounded(prefix_weights), base_values, precision=strict_setting)
        numerator = numerator + jnp.einsum('bsgc,bcd->bsgd', rounded(page_weights), page_values, precision=strict_setting)
        numerator = numerator + jnp.einsum('bsgu,bud->bsgd', rounded(new_weights), new_values, precision=strict_setting)
        denominator = jnp.sum(prefix_weights, axis=3) + jnp.sum(page_weights, axis=3) + jnp.sum(new_weights, axis=3)
        return numerator / denominator[..., None]

    per_head = lax.map(one_head, jnp.arange(KVH, dtype=jnp.int32))
    return jnp.transpose(per_head, (1, 2, 0, 3, 4)).reshape(row_count, STEPS, QH * HD).astype(jnp.bfloat16)
```

```python
import functools
import math

import jax
import jax.numpy as jnp
from jax import lax
from jax.experimental import pallas as pl
from jax.experimental.pallas import tpu as pltpu
from jax.sharding import PartitionSpec as P

QH = 64
KVH = 8
HD = 128
GROUP = QH // KVH
CHUNKS = 4
HC = KVH // CHUNKS
FAR = -1e30
COEF = HD**-0.5 * math.log2(math.e)


def kernel(
    n,
    table_ref,
    offsets_ref,
    lengths_ref,
    q_ref,
    new_ref,
    base_hbm,
    pool_hbm,
    out_ref,
    kv,
    limits,
    spread,
    gathered,
    part,
    part_ml,
    core_in,
    core_in_ml,
    yhalf,
    yhalf_ml,
    y_in,
    y_in_ml,
    zsend,
    zsend_ml,
    z_in,
    z_in_ml,
    factors,
    load_sem,
    gz_send,
    gz_recv,
    gy_send,
    gy_recv,
    gc_send,
    gc_recv,
    rc_send,
    rc_recv,
    ry_send,
    ry_recv,
    rz_send,
    rz_recv,
):
    steps = q_ref.shape[1]
    block = GROUP * steps
    planes = n // 4
    quarter = planes * block
    lanes = n * block
    base_len = base_hbm.shape[0]
    pages_here, page_len, _ = pool_hbm.shape
    rows, slots = table_ref.shape
    pages_at = base_len
    new_at = base_len + pages_here * page_len
    new_pad = kv.shape[0] - new_at

    me = lax.axis_index("seq")
    core = lax.rem(me, 2)
    y = lax.rem(lax.div(me, 2), 2)
    plane = lax.div(me, 4)
    position = core * (2 * planes) + y * planes + plane
    core_peer = plane * 4 + y * 2 + (1 - core)
    y_peer = plane * 4 + (1 - y) * 2 + core

    def plane_at(j):
        return lax.rem(plane + j, planes)

    def plane_before(j):
        return lax.rem(plane + planes - j, planes)

    def z_peer(j):
        return plane_at(j) * 4 + y * 2 + core

    loads = [pltpu.make_async_copy(base_hbm, kv.at[pl.ds(0, base_len)], load_sem.at[0])]
    for p in range(pages_here):
        loads.append(
            pltpu.make_async_copy(
                pool_hbm.at[p],
                kv.at[pl.ds(pages_at + p * page_len, page_len)],
                load_sem.at[1 + p],
            )
        )
    for load in loads:
        load.start()

    barrier = pltpu.get_barrier_semaphore()
    peers = [core_peer, y_peer] + [z_peer(j) for j in range(1, planes)]
    for peer in peers:
        pl.semaphore_signal(
            barrier, inc=1, device_id={"seq": peer}, device_id_type=pl.DeviceIdType.MESH
        )

    wide = q_ref[0].astype(jnp.float32)
    for i in range(QH):
        spread[i * steps : (i + 1) * steps, :] = wide[:, i * HD : (i + 1) * HD]
    own = spread[...].astype(jnp.bfloat16)
    own_at = pl.multiple_of(position * block, block)
    for h in range(KVH):
        gathered[h, pl.ds(own_at, block), :] = own[h * block : (h + 1) * block, :]

    pl.semaphore_wait(barrier, len(peers))

    def remote(src, dst, send, recv, peer):
        return pltpu.make_async_remote_copy(
            src_ref=src,
            dst_ref=dst,
            send_sem=send,
            recv_sem=recv,
            device_id={"seq": peer},
            device_id_type=pl.DeviceIdType.MESH,
        )

    def rows_of(c, first, count):
        return gathered.at[
            pl.ds(c * HC, HC), pl.ds(pl.multiple_of(first * block, block), count * block)
        ]

    def gather_z(c, j):
        ref = rows_of(c, position, 1)
        return remote(ref, ref, gz_send.at[c, j - 1], gz_recv.at[c, j - 1], z_peer(j))

    def gather_z_in(c, j):
        ref = rows_of(c, core * (2 * planes) + y * planes + plane_before(j), 1)
        return remote(ref, ref, gz_send.at[c, j - 1], gz_recv.at[c, j - 1], z_peer(j))

    def gather_y(c):
        ref = rows_of(c, core * (2 * planes) + y * planes, planes)
        return remote(ref, ref, gy_send.at[c], gy_recv.at[c], y_peer)

    def gather_y_in(c):
        ref = rows_of(c, core * (2 * planes) + (1 - y) * planes, planes)
        return remote(ref, ref, gy_send.at[c], gy_recv.at[c], y_peer)

    def gather_core(c, which):
        yy = y if which == 0 else 1 - y
        ref = rows_of(c, core * (2 * planes) + yy * planes, planes)
        return remote(ref, ref, gc_send.at[c, which], gc_recv.at[c, which], core_peer)

    def gather_core_in(c, which):
        yy = y if which == 0 else 1 - y
        ref = rows_of(c, (1 - core) * (2 * planes) + yy * planes, planes)
        return remote(ref, ref, gc_send.at[c, which], gc_recv.at[c, which], core_peer)

    def core_copies(c):
        theirs = pl.ds((1 - core) * 2, 2)
        return (
            remote(part.at[c, theirs], core_in.at[c], rc_send.at[c, 0], rc_recv.at[c, 0], core_peer),
            remote(
                part_ml.at[c, theirs], core_in_ml.at[c], rc_send.at[c, 1], rc_recv.at[c, 1], core_peer
            ),
        )

    def y_copies(c):
        return (
            remote(yhalf.at[c, 1 - y], y_in.at[c], ry_send.at[c, 0], ry_recv.at[c, 0], y_peer),
            remote(yhalf_ml.at[c, 1 - y], y_in_ml.at[c], ry_send.at[c, 1], ry_recv.at[c, 1], y_peer),
        )

    def z_copies(c, j):
        theirs = pl.ds(pl.multiple_of(plane_at(j) * block, block), block)
        return (
            remote(
                zsend.at[c, :, theirs],
                z_in.at[c, j - 1],
                rz_send.at[c, j - 1, 0],
                rz_recv.at[c, j - 1, 0],
                z_peer(j),
            ),
            remote(
                zsend_ml.at[c],
                z_in_ml.at[c, j - 1],
                rz_send.at[c, j - 1, 1],
                rz_recv.at[c, j - 1, 1],
                z_peer(j),
            ),
        )

    for c in range(CHUNKS):
        for j in range(1, planes):
            gather_z(c, j).start()

    lane = lax.broadcasted_iota(jnp.int32, (1, lanes), 1)
    lane_block = lax.div(lane, block)
    base_limit = jnp.zeros((1, lanes), jnp.int32)
    page_limits = [jnp.zeros((1, lanes), jnp.int32) for _ in range(pages_here)]
    for b in range(rows):
        at = (b % 2) * (2 * planes) + (b // 2 % 2) * planes + b // 4
        here = lane_block == at
        base_limit = jnp.where(here, offsets_ref[b] - me * base_len, base_limit)
        for p in range(pages_here):
            live = jnp.int32(0)
            for s in range(slots):
                live = live + jnp.where(
                    table_ref[b, s] == me * pages_here + p, lengths_ref[b] - s * page_len, 0
                )
            page_limits[p] = jnp.where(here, live, page_limits[p])
    new_limit = jnp.where(lane_block == position, lax.rem(lane, steps) + 1, 0)
    for i, limit in enumerate([base_limit] + page_limits + [new_limit]):
        limits[i : i + 1, :] = limit
    kv[new_at:, :] = jnp.concatenate(
        [new_ref[0].astype(jnp.float32), jnp.zeros((new_pad - steps, kv.shape[1]), jnp.float32)],
        axis=0,
    ).astype(jnp.bfloat16)

    key_blocks = [(0, base_len)]
    key_blocks += [(pages_at + p * page_len, page_len) for p in range(pages_here)]
    key_blocks += [(new_at, new_pad)]
    width = min(lanes, 512)
    per_width = width // quarter

    def forward_first(c):
        for j in range(1, planes):
            gather_z_in(c, j).wait_recv()
        gather_y(c).start()
        gather_core(c, 0).start()

    def forward_second(c):
        gather_y_in(c).wait_recv()
        gather_core(c, 1).start()

    def attend(c):
        gather_core_in(c, 0).wait_recv()
        gather_core_in(c, 1).wait_recv()

        def lane_part(lb):
            start = pl.multiple_of(lb * width, width)
            tops, totals = [], []
            for hh in range(HC):
                h = c * HC + hh
                queries = gathered[h, pl.ds(start, width), :]
                keys = kv[:, 2 * h * HD : (2 * h + 1) * HD]
                values = kv[:, (2 * h + 1) * HD : (2 * h + 2) * HD]
                scores = lax.dot_general(
                    keys, queries, (((1,), (1,)), ((), ())), preferred_element_type=jnp.float32
                )
                pieces = []
                for i, (at, count) in enumerate(key_blocks):
                    key = lax.broadcasted_iota(jnp.int32, (count, width), 0)
                    limit = limits[i : i + 1, pl.ds(start, width)]
                    pieces.append(jnp.where(key < limit, scores[at : at + count], FAR))
                top = functools.reduce(
                    jnp.maximum, [jnp.max(x, axis=0, keepdims=True) for x in pieces]
                )
                weights = [jnp.exp2((x - top) * COEF) for x in pieces]
                total = sum(jnp.sum(x, axis=0, keepdims=True) for x in weights)
                rounded = jnp.concatenate([x.astype(jnp.bfloat16) for x in weights], axis=0)
                sums = lax.dot_general(
                    values, rounded, (((0,), (0,)), ((), ())), preferred_element_type=jnp.float32
                ).astype(jnp.bfloat16)
                for i in range(per_width):
                    part[c, lb * per_width + i, hh] = sums[:, i * quarter : (i + 1) * quarter]
                tops.append(top)
                totals.append(total)
            pad = [jnp.zeros((4 - HC, width), jnp.float32)] if HC < 4 else []
            both = jnp.concatenate(tops + pad + totals + pad, axis=0)
            for i in range(per_width):
                part_ml[c, lb * per_width + i] = both[:, i * quarter : (i + 1) * quarter]

        if lanes == width:
            lane_part(0)
        else:
            lax.fori_loop(0, lanes // width, lambda lb, _: (lane_part(lb), 0)[1], 0)
        for copy in core_copies(c):
            copy.start()

    def merge_ml(mine, theirs):
        top = jnp.maximum(mine[:4], theirs[:4])
        a = jnp.exp2((mine[:4] - top) * COEF)
        b = jnp.exp2((theirs[:4] - top) * COEF)
        return a, b, jnp.concatenate([top, a * mine[4:] + b * theirs[4:]], axis=0)

    def merge_core(c):
        for copy in core_copies(c):
            copy.wait_recv()
        for yy in range(2):
            a, b, ml = merge_ml(part_ml[c, core * 2 + yy], core_in_ml[c, yy])
            yhalf_ml[c, yy] = ml
            for hh in range(HC):
                merged = part[c, core * 2 + yy, hh].astype(jnp.float32) * a[hh : hh + 1]
                merged = merged + core_in[c, yy, hh].astype(jnp.float32) * b[hh : hh + 1]
                yhalf[c, yy, hh] = merged.astype(jnp.bfloat16)
        for copy in y_copies(c):
            copy.start()

    def merge_y(c):
        for copy in y_copies(c):
            copy.wait_recv()
        a, b, ml = merge_ml(yhalf_ml[c, y], y_in_ml[c])
        zsend_ml[c] = ml
        for hh in range(HC):
            merged = yhalf[c, y, hh].astype(jnp.float32) * a[hh : hh + 1]
            merged = merged + y_in[c, hh].astype(jnp.float32) * b[hh : hh + 1]
            zsend[c, hh] = merged.T.astype(jnp.bfloat16)
        for j in range(1, planes):
            for copy in z_copies(c, j):
                copy.start()

    def finish(c):
        for j in range(1, planes):
            for copy in z_copies(c, j):
                copy.wait_recv()
        parts = [zsend_ml[c]] + [z_in_ml[c, j - 1] for j in range(1, planes)]
        top = functools.reduce(jnp.maximum, [x[:4] for x in parts])
        scales = [jnp.exp2((x[:4] - top) * COEF) for x in parts]
        total = sum(s * x[4:] for s, x in zip(scales, parts))
        scales = [s / total if HC == 4 else s[:HC] / total[:HC] for s in scales]
        pad = [jnp.zeros((HD - planes * HC, quarter), jnp.float32)]
        factors[c] = jnp.concatenate(scales + pad, axis=0).T
        mine = pl.ds(pl.multiple_of(plane * block, block), block)
        by_source = factors[c, mine, :]
        for hh in range(HC):
            h = c * HC + hh
            result = zsend[c, hh, mine, :].astype(jnp.float32) * by_source[:, hh : hh + 1]
            for j in range(1, planes):
                at = j * HC + hh
                result = result + z_in[c, j - 1, hh].astype(jnp.float32) * by_source[:, at : at + 1]
            for g in range(GROUP):
                at = (h * GROUP + g) * HD
                out_ref[0, :, at : at + HD] = result[g * steps : (g + 1) * steps, :].astype(
                    jnp.bfloat16
                )

    for t in range(CHUNKS + 5):
        if 0 <= t < CHUNKS:
            forward_first(t)
        if 0 <= t - 1 < CHUNKS:
            forward_second(t - 1)
        if t == 2:
            for load in loads:
                load.wait()
        if 0 <= t - 2 < CHUNKS:
            attend(t - 2)
        if 0 <= t - 3 < CHUNKS:
            merge_core(t - 3)
        if 0 <= t - 4 < CHUNKS:
            merge_y(t - 4)
        if 0 <= t - 5 < CHUNKS:
            finish(t - 5)

    for c in range(CHUNKS):
        for j in range(1, planes):
            gather_z(c, j).wait_send()
            for copy in z_copies(c, j):
                copy.wait_send()
        gather_y(c).wait_send()
        gather_core(c, 0).wait_send()
        gather_core(c, 1).wait_send()
        for copy in core_copies(c) + y_copies(c):
            copy.wait_send()


def body(n, queries, base_cache, page_pool, new_cache, page_table, offsets, lengths):
    steps = queries.shape[1]
    block = GROUP * steps
    planes = n // 4
    quarter = planes * block
    lanes = n * block
    pages_here, page_len, columns = page_pool.shape
    keys = base_cache.shape[0] + pages_here * page_len + 16
    bf16, f32 = jnp.bfloat16, jnp.float32
    dma = pltpu.SemaphoreType.DMA
    smem = pl.BlockSpec(memory_space=pltpu.SMEM)
    vmem = pl.BlockSpec(memory_space=pltpu.VMEM)
    hbm = pl.BlockSpec(memory_space=pl.ANY)
    return pl.pallas_call(
        functools.partial(kernel, n),
        out_shape=jax.ShapeDtypeStruct(queries.shape, bf16),
        in_specs=[smem, smem, smem, vmem, vmem, hbm, hbm],
        out_specs=vmem,
        scratch_shapes=[
            pltpu.VMEM((keys, columns), bf16),
            pltpu.VMEM((max(8, pages_here + 2), lanes), jnp.int32),
            pltpu.VMEM((QH * steps, HD), f32),
            pltpu.VMEM((KVH, lanes, HD), bf16),
            pltpu.VMEM((CHUNKS, 4, HC, HD, quarter), bf16),
            pltpu.VMEM((CHUNKS, 4, 8, quarter), f32),
            pltpu.VMEM((CHUNKS, 2, HC, HD, quarter), bf16),
            pltpu.VMEM((CHUNKS, 2, 8, quarter), f32),
            pltpu.VMEM((CHUNKS, 2, HC, HD, quarter), bf16),
            pltpu.VMEM((CHUNKS, 2, 8, quarter), f32),
            pltpu.VMEM((CHUNKS, HC, HD, quarter), bf16),
            pltpu.VMEM((CHUNKS, 8, quarter), f32),
            pltpu.VMEM((CHUNKS, HC, quarter, HD), bf16),
            pltpu.VMEM((CHUNKS, 8, quarter), f32),
            pltpu.VMEM((CHUNKS, planes - 1, HC, block, HD), bf16),
            pltpu.VMEM((CHUNKS, planes - 1, 8, quarter), f32),
            pltpu.VMEM((CHUNKS, quarter, HD), f32),
            dma((1 + pages_here,)),
            dma((CHUNKS, planes - 1)),
            dma((CHUNKS, planes - 1)),
            dma((CHUNKS,)),
            dma((CHUNKS,)),
            dma((CHUNKS, 2)),
            dma((CHUNKS, 2)),
            dma((CHUNKS, 2)),
            dma((CHUNKS, 2)),
            dma((CHUNKS, 2)),
            dma((CHUNKS, 2)),
            dma((CHUNKS, planes - 1, 2)),
            dma((CHUNKS, planes - 1, 2)),
        ],
        compiler_params=pltpu.CompilerParams(
            collective_id=0, has_side_effects=True, vmem_limit_bytes=56 * 1024 * 1024
        ),
    )(page_table, offsets, lengths, queries, new_cache, base_cache, page_pool)


def solution(mesh):
    in_specs = (
        P(("groups", "seq"), None, None),
        P(("groups", "seq"), None),
        P(("groups", "seq"), None, None),
        P(("groups", "seq"), None, None),
        P("groups", None),
        P("groups"),
        P("groups"),
    )
    return jax.shard_map(
        functools.partial(body, mesh.shape["seq"]),
        mesh=mesh,
        in_specs=in_specs,
        out_specs=P(("groups", "seq"), None, None),
        check_vma=False,
    )
```

```python
import functools
import math

import jax
import jax.numpy as jnp
from jax import lax
from jax.experimental import pallas as pl
from jax.experimental.pallas import tpu as pltpu
from jax.sharding import PartitionSpec as P

QH = 64
KVH = 8
HD = 128
GROUP = QH // KVH
CHUNKS = 4
HC = KVH // CHUNKS
SCHEDULE = [
    ("gather z", 0),
    ("gather z", 1),
    ("gather y", 0),
    ("gather z", 2),
    ("gather y", 1),
    ("attend", 0),
    ("gather z", 3),
    ("gather y", 2),
    ("attend", 1),
    ("core", 0),
    ("gather y", 3),
    ("attend", 2),
    ("core", 1),
    ("y", 0),
    ("attend", 3),
    ("core", 2),
    ("y", 1),
    ("core", 3),
    ("y", 2),
    ("z", 0),
    ("y", 3),
    ("z", 1),
    ("z", 2),
    ("z", 3),
]
FAR = -1e30
COEF = HD**-0.5 * math.log2(math.e)


def kernel(
    n,
    table_ref,
    offsets_ref,
    lengths_ref,
    q_ref,
    new_ref,
    base_hbm,
    pool_hbm,
    out_ref,
    kv,
    limits,
    spread,
    gathered,
    part,
    part_ml,
    core_in,
    core_in_ml,
    yhalf,
    yhalf_ml,
    y_in,
    y_in_ml,
    zsend,
    zsend_ml,
    z_in,
    z_in_ml,
    factors,
    load_sem,
    gz_send,
    gz_recv,
    gy_send,
    gy_recv,
    gc_send,
    gc_recv,
    rc_send,
    rc_recv,
    ry_send,
    ry_recv,
    rz_send,
    rz_recv,
):
    steps = q_ref.shape[1]
    block = GROUP * steps
    planes = n // 4
    quarter = planes * block
    lanes = n * block
    base_len = base_hbm.shape[0]
    pages_here, page_len, _ = pool_hbm.shape
    slots, rows = table_ref.shape
    pages_at = base_len
    new_at = base_len + pages_here * page_len
    new_pad = kv.shape[0] - new_at

    me = lax.axis_index("seq")
    core = lax.rem(me, 2)
    y = lax.rem(lax.div(me, 2), 2)
    plane = lax.div(me, 4)
    position = core * (2 * planes) + y * planes + plane
    core_peer = plane * 4 + y * 2 + (1 - core)
    y_peer = plane * 4 + (1 - y) * 2 + core

    def plane_at(j):
        return lax.rem(plane + j, planes)

    def plane_before(j):
        return lax.rem(plane + planes - j, planes)

    def z_peer(j):
        return plane_at(j) * 4 + y * 2 + core

    loads = [pltpu.make_async_copy(base_hbm, kv.at[pl.ds(0, base_len)], load_sem.at[0])]
    for p in range(pages_here):
        loads.append(
            pltpu.make_async_copy(
                pool_hbm.at[p],
                kv.at[pl.ds(pages_at + p * page_len, page_len)],
                load_sem.at[1 + p],
            )
        )
    for load in loads:
        load.start()

    barrier = pltpu.get_barrier_semaphore()
    peers = [core_peer, y_peer] + [z_peer(j) for j in range(1, planes)]
    for peer in peers:
        pl.semaphore_signal(
            barrier, inc=1, device_id={"seq": peer}, device_id_type=pl.DeviceIdType.MESH
        )

    wide = q_ref[0].astype(jnp.float32)
    for i in range(QH):
        spread[i * steps : (i + 1) * steps, :] = wide[:, i * HD : (i + 1) * HD]
    own = spread[...].astype(jnp.bfloat16)
    own_at = pl.multiple_of(position * block, block)
    for h in range(KVH):
        gathered[h, pl.ds(own_at, block), :] = own[h * block : (h + 1) * block, :]

    pl.semaphore_wait(barrier, len(peers))

    def remote(src, dst, send, recv, peer):
        return pltpu.make_async_remote_copy(
            src_ref=src,
            dst_ref=dst,
            send_sem=send,
            recv_sem=recv,
            device_id={"seq": peer},
            device_id_type=pl.DeviceIdType.MESH,
        )

    def rows_of(c, first, count):
        return gathered.at[
            pl.ds(c * HC, HC), pl.ds(pl.multiple_of(first * block, block), count * block)
        ]

    def gather_z(c, j):
        ref = rows_of(c, position, 1)
        return remote(ref, ref, gz_send.at[c, j - 1], gz_recv.at[c, j - 1], z_peer(j))

    def gather_z_in(c, j):
        ref = rows_of(c, core * (2 * planes) + y * planes + plane_before(j), 1)
        return remote(ref, ref, gz_send.at[c, j - 1], gz_recv.at[c, j - 1], z_peer(j))

    def gather_y(c):
        ref = rows_of(c, core * (2 * planes) + y * planes, planes)
        return remote(ref, ref, gy_send.at[c], gy_recv.at[c], y_peer)

    def gather_y_in(c):
        ref = rows_of(c, core * (2 * planes) + (1 - y) * planes, planes)
        return remote(ref, ref, gy_send.at[c], gy_recv.at[c], y_peer)

    def gather_core(c, which):
        yy = y if which == 0 else 1 - y
        ref = rows_of(c, core * (2 * planes) + yy * planes, planes)
        return remote(ref, ref, gc_send.at[c, which], gc_recv.at[c, which], core_peer)

    def gather_core_in(c, which):
        yy = y if which == 0 else 1 - y
        ref = rows_of(c, (1 - core) * (2 * planes) + yy * planes, planes)
        return remote(ref, ref, gc_send.at[c, which], gc_recv.at[c, which], core_peer)

    def core_copies(c):
        theirs = pl.ds((1 - core) * 2, 2)
        return (
            remote(part.at[c, theirs], core_in.at[c], rc_send.at[c, 0], rc_recv.at[c, 0], core_peer),
            remote(
                part_ml.at[c, theirs], core_in_ml.at[c], rc_send.at[c, 1], rc_recv.at[c, 1], core_peer
            ),
        )

    def y_copies(c):
        return (
            remote(yhalf.at[c, 1 - y], y_in.at[c], ry_send.at[c, 0], ry_recv.at[c, 0], y_peer),
            remote(yhalf_ml.at[c, 1 - y], y_in_ml.at[c], ry_send.at[c, 1], ry_recv.at[c, 1], y_peer),
        )

    def z_copies(c, j):
        theirs = pl.ds(pl.multiple_of(plane_at(j) * block, block), block)
        return (
            remote(
                zsend.at[c, :, theirs],
                z_in.at[c, j - 1],
                rz_send.at[c, j - 1, 0],
                rz_recv.at[c, j - 1, 0],
                z_peer(j),
            ),
            remote(
                zsend_ml.at[c],
                z_in_ml.at[c, j - 1],
                rz_send.at[c, j - 1, 1],
                rz_recv.at[c, j - 1, 1],
                z_peer(j),
            ),
        )

    for c in range(2):
        for j in range(1, planes):
            gather_z(c, j).start()

    lane = lax.broadcasted_iota(jnp.int32, (1, lanes), 1)
    lane_block = lax.div(lane, block)
    base_limit = jnp.zeros((1, lanes), jnp.int32)
    page_limits = [jnp.zeros((1, lanes), jnp.int32) for _ in range(pages_here)]
    for b in range(rows):
        at = (b % 2) * (2 * planes) + (b // 2 % 2) * planes + b // 4
        here = lane_block == at
        base_limit = jnp.where(here, offsets_ref[b] - me * base_len, base_limit)
        for p in range(pages_here):
            live = jnp.int32(0)
            for s in range(slots):
                live = live + jnp.where(
                    table_ref[s, b] == me * pages_here + p, lengths_ref[b] - s * page_len, 0
                )
            page_limits[p] = jnp.where(here, live, page_limits[p])
    new_limit = jnp.where(lane_block == position, lax.rem(lane, steps) + 1, 0)
    for i, limit in enumerate([base_limit] + page_limits + [new_limit]):
        limits[i : i + 1, :] = limit
    kv[new_at:, :] = jnp.concatenate(
        [new_ref[0].astype(jnp.float32), jnp.zeros((new_pad - steps, kv.shape[1]), jnp.float32)],
        axis=0,
    ).astype(jnp.bfloat16)

    key_blocks = [(0, base_len)]
    key_blocks += [(pages_at + p * page_len, page_len) for p in range(pages_here)]
    key_blocks += [(new_at, new_pad)]
    width = min(lanes, 512)
    per_width = width // quarter

    def forward_first(c):
        for j in range(1, planes):
            gather_z_in(c, j).wait_recv()
            if c + 2 < CHUNKS:
                gather_z(c + 2, j).start()
        gather_y(c).start()
        gather_core(c, 0).start()

    def forward_second(c):
        gather_y_in(c).wait_recv()
        gather_core(c, 1).start()

    def attend(c):
        gather_core_in(c, 0).wait_recv()
        gather_core_in(c, 1).wait_recv()

        def lane_part(lb):
            start = pl.multiple_of(lb * width, width)
            tops, totals = [], []
            for hh in range(HC):
                h = c * HC + hh
                queries = gathered[h, pl.ds(start, width), :]
                keys = kv[:, 2 * h * HD : (2 * h + 1) * HD]
                values = kv[:, (2 * h + 1) * HD : (2 * h + 2) * HD]
                scores = lax.dot_general(
                    keys, queries, (((1,), (1,)), ((), ())), preferred_element_type=jnp.float32
                )
                pieces = []
                for i, (at, count) in enumerate(key_blocks):
                    key = lax.broadcasted_iota(jnp.int32, (count, width), 0)
                    limit = limits[i : i + 1, pl.ds(start, width)]
                    pieces.append(jnp.where(key < limit, scores[at : at + count], FAR))
                top = functools.reduce(
                    jnp.maximum, [jnp.max(x, axis=0, keepdims=True) for x in pieces]
                )
                weights = [jnp.exp2((x - top) * COEF) for x in pieces]
                total = sum(jnp.sum(x, axis=0, keepdims=True) for x in weights)
                rounded = jnp.concatenate([x.astype(jnp.bfloat16) for x in weights], axis=0)
                sums = lax.dot_general(
                    values, rounded, (((0,), (0,)), ((), ())), preferred_element_type=jnp.float32
                ).astype(jnp.bfloat16)
                for i in range(per_width):
                    part[c, lb * per_width + i, hh] = sums[:, i * quarter : (i + 1) * quarter]
                tops.append(top)
                totals.append(total)
            pad = [jnp.zeros((4 - HC, width), jnp.float32)] if HC < 4 else []
            both = jnp.concatenate(tops + pad + totals + pad, axis=0)
            for i in range(per_width):
                part_ml[c, lb * per_width + i] = both[:, i * quarter : (i + 1) * quarter]

        if lanes == width:
            lane_part(0)
        else:
            lax.fori_loop(0, lanes // width, lambda lb, _: (lane_part(lb), 0)[1], 0)
        for copy in core_copies(c):
            copy.start()

    def merge_ml(mine, theirs):
        top = jnp.maximum(mine[:4], theirs[:4])
        a = jnp.exp2((mine[:4] - top) * COEF)
        b = jnp.exp2((theirs[:4] - top) * COEF)
        return a, b, jnp.concatenate([top, a * mine[4:] + b * theirs[4:]], axis=0)

    def merge_core(c):
        for copy in core_copies(c):
            copy.wait_recv()
        for yy in range(2):
            a, b, ml = merge_ml(part_ml[c, core * 2 + yy], core_in_ml[c, yy])
            yhalf_ml[c, yy] = ml
            for hh in range(HC):
                merged = part[c, core * 2 + yy, hh].astype(jnp.float32) * a[hh : hh + 1]
                merged = merged + core_in[c, yy, hh].astype(jnp.float32) * b[hh : hh + 1]
                yhalf[c, yy, hh] = merged.astype(jnp.bfloat16)
        for copy in y_copies(c):
            copy.start()

    def merge_y(c):
        for copy in y_copies(c):
            copy.wait_recv()
        a, b, ml = merge_ml(yhalf_ml[c, y], y_in_ml[c])
        zsend_ml[c] = ml
        for hh in range(HC):
            merged = yhalf[c, y, hh].astype(jnp.float32) * a[hh : hh + 1]
            merged = merged + y_in[c, hh].astype(jnp.float32) * b[hh : hh + 1]
            zsend[c, hh] = merged.T.astype(jnp.bfloat16)
        for j in range(1, planes):
            for copy in z_copies(c, j):
                copy.start()

    def finish(c):
        for j in range(1, planes):
            for copy in z_copies(c, j):
                copy.wait_recv()
        parts = [zsend_ml[c]] + [z_in_ml[c, j - 1] for j in range(1, planes)]
        top = functools.reduce(jnp.maximum, [x[:4] for x in parts])
        scales = [jnp.exp2((x[:4] - top) * COEF) for x in parts]
        total = sum(s * x[4:] for s, x in zip(scales, parts))
        scales = [s / total if HC == 4 else s[:HC] / total[:HC] for s in scales]
        pad = [jnp.zeros((HD - planes * HC, quarter), jnp.float32)]
        factors[c] = jnp.concatenate(scales + pad, axis=0).T
        mine = pl.ds(pl.multiple_of(plane * block, block), block)
        by_source = factors[c, mine, :]
        for hh in range(HC):
            h = c * HC + hh
            result = zsend[c, hh, mine, :].astype(jnp.float32) * by_source[:, hh : hh + 1]
            for j in range(1, planes):
                at = j * HC + hh
                result = result + z_in[c, j - 1, hh].astype(jnp.float32) * by_source[:, at : at + 1]
            for g in range(GROUP):
                at = (h * GROUP + g) * HD
                out_ref[0, :, at : at + HD] = result[g * steps : (g + 1) * steps, :].astype(
                    jnp.bfloat16
                )

    stages = {
        "gather z": forward_first,
        "gather y": forward_second,
        "attend": attend,
        "core": merge_core,
        "y": merge_y,
        "z": finish,
    }
    loaded = False
    for stage, c in SCHEDULE:
        if stage == "attend" and not loaded:
            loaded = True
            for load in loads:
                load.wait()
        stages[stage](c)

    for c in range(CHUNKS):
        for j in range(1, planes):
            gather_z(c, j).wait_send()
            for copy in z_copies(c, j):
                copy.wait_send()
        gather_y(c).wait_send()
        gather_core(c, 0).wait_send()
        gather_core(c, 1).wait_send()
        for copy in core_copies(c) + y_copies(c):
            copy.wait_send()


def body(n, queries, base_cache, page_pool, new_cache, page_table, offsets, lengths):
    steps = queries.shape[1]
    block = GROUP * steps
    planes = n // 4
    quarter = planes * block
    lanes = n * block
    pages_here, page_len, columns = page_pool.shape
    keys = base_cache.shape[0] + pages_here * page_len + 16
    bf16, f32 = jnp.bfloat16, jnp.float32
    dma = pltpu.SemaphoreType.DMA
    smem = pl.BlockSpec(memory_space=pltpu.SMEM)
    vmem = pl.BlockSpec(memory_space=pltpu.VMEM)
    hbm = pl.BlockSpec(memory_space=pl.ANY)
    return pl.pallas_call(
        functools.partial(kernel, n),
        out_shape=jax.ShapeDtypeStruct(queries.shape, bf16),
        in_specs=[smem, smem, smem, vmem, vmem, hbm, hbm],
        out_specs=vmem,
        scratch_shapes=[
            pltpu.VMEM((keys, columns), bf16),
            pltpu.VMEM((max(8, pages_here + 2), lanes), jnp.int32),
            pltpu.VMEM((QH * steps, HD), f32),
            pltpu.VMEM((KVH, lanes, HD), bf16),
            pltpu.VMEM((CHUNKS, 4, HC, HD, quarter), bf16),
            pltpu.VMEM((CHUNKS, 4, 8, quarter), f32),
            pltpu.VMEM((CHUNKS, 2, HC, HD, quarter), bf16),
            pltpu.VMEM((CHUNKS, 2, 8, quarter), f32),
            pltpu.VMEM((CHUNKS, 2, HC, HD, quarter), bf16),
            pltpu.VMEM((CHUNKS, 2, 8, quarter), f32),
            pltpu.VMEM((CHUNKS, HC, HD, quarter), bf16),
            pltpu.VMEM((CHUNKS, 8, quarter), f32),
            pltpu.VMEM((CHUNKS, HC, quarter, HD), bf16),
            pltpu.VMEM((CHUNKS, 8, quarter), f32),
            pltpu.VMEM((CHUNKS, planes - 1, HC, block, HD), bf16),
            pltpu.VMEM((CHUNKS, planes - 1, 8, quarter), f32),
            pltpu.VMEM((CHUNKS, quarter, HD), f32),
            dma((1 + pages_here,)),
            dma((CHUNKS, planes - 1)),
            dma((CHUNKS, planes - 1)),
            dma((CHUNKS,)),
            dma((CHUNKS,)),
            dma((CHUNKS, 2)),
            dma((CHUNKS, 2)),
            dma((CHUNKS, 2)),
            dma((CHUNKS, 2)),
            dma((CHUNKS, 2)),
            dma((CHUNKS, 2)),
            dma((CHUNKS, planes - 1, 2)),
            dma((CHUNKS, planes - 1, 2)),
        ],
        compiler_params=pltpu.CompilerParams(
            collective_id=0, has_side_effects=True, vmem_limit_bytes=56 * 1024 * 1024
        ),
    )(page_table.T, offsets, lengths, queries, new_cache, base_cache, page_pool)


def solution(mesh):
    in_specs = (
        P(("groups", "seq"), None, None),
        P(("groups", "seq"), None),
        P(("groups", "seq"), None, None),
        P(("groups", "seq"), None, None),
        P("groups", None),
        P("groups"),
        P("groups"),
    )
    return jax.shard_map(
        functools.partial(body, mesh.shape["seq"]),
        mesh=mesh,
        in_specs=in_specs,
        out_specs=P(("groups", "seq"), None, None),
        check_vma=False,
    )
```

```python
import functools
import math

import jax
import jax.numpy as jnp
from jax import lax
from jax.experimental import pallas as pl
from jax.experimental.pallas import tpu as pltpu
from jax.sharding import PartitionSpec as P

QH = 64
KVH = 8
HD = 128
GROUP = QH // KVH
CHUNKS = 4
HC = KVH // CHUNKS
SCHEDULE = [
    ("gather z", 0),
    ("gather z", 1),
    ("gather y", 0),
    ("gather z", 2),
    ("gather y", 1),
    ("attend", 0),
    ("gather z", 3),
    ("gather y", 2),
    ("attend", 1),
    ("core", 0),
    ("gather y", 3),
    ("attend", 2),
    ("core", 1),
    ("y", 0),
    ("attend", 3),
    ("core", 2),
    ("y", 1),
    ("core", 3),
    ("y", 2),
    ("z", 0),
    ("y", 3),
    ("z", 1),
    ("z", 2),
    ("z", 3),
]
FAR = -1e30
COEF = HD**-0.5 * math.log2(math.e)


def kernel(
    n,
    table_ref,
    offsets_ref,
    lengths_ref,
    q_ref,
    new_ref,
    base_hbm,
    pool_hbm,
    out_ref,
    kv,
    limits,
    spread,
    gathered,
    part,
    part_ml,
    core_in,
    core_in_ml,
    yhalf,
    yhalf_ml,
    y_in,
    y_in_ml,
    zsend,
    zsend_ml,
    z_in,
    z_in_ml,
    factors,
    load_sem,
    gz_send,
    gz_recv,
    gy_send,
    gy_recv,
    gc_send,
    gc_recv,
    rc_send,
    rc_recv,
    ry_send,
    ry_recv,
    rz_send,
    rz_recv,
):
    steps = q_ref.shape[1]
    block = GROUP * steps
    planes = n // 4
    quarter = planes * block
    lanes = n * block
    base_len = base_hbm.shape[0]
    pages_here, page_len, _ = pool_hbm.shape
    slots, rows = table_ref.shape
    pages_at = base_len
    new_at = base_len + pages_here * page_len
    new_pad = kv.shape[0] - new_at

    me = lax.axis_index("seq")
    core = lax.rem(me, 2)
    y = lax.rem(lax.div(me, 2), 2)
    plane = lax.div(me, 4)
    position = core * (2 * planes) + y * planes + plane
    core_peer = plane * 4 + y * 2 + (1 - core)
    y_peer = plane * 4 + (1 - y) * 2 + core

    def plane_at(j):
        return lax.rem(plane + j, planes)

    def plane_before(j):
        return lax.rem(plane + planes - j, planes)

    def z_peer(j):
        return plane_at(j) * 4 + y * 2 + core

    loads = [pltpu.make_async_copy(base_hbm, kv.at[pl.ds(0, base_len)], load_sem.at[0])]
    for p in range(pages_here):
        loads.append(
            pltpu.make_async_copy(
                pool_hbm.at[p],
                kv.at[pl.ds(pages_at + p * page_len, page_len)],
                load_sem.at[1 + p],
            )
        )
    for load in loads:
        load.start()

    barrier = pltpu.get_barrier_semaphore()
    peers = [core_peer, y_peer] + [z_peer(j) for j in range(1, planes)]
    for peer in peers:
        pl.semaphore_signal(
            barrier, inc=1, device_id={"seq": peer}, device_id_type=pl.DeviceIdType.MESH
        )

    wide = q_ref[0].astype(jnp.float32)
    for i in range(QH):
        spread[i * steps : (i + 1) * steps, :] = wide[:, i * HD : (i + 1) * HD]
    own = spread[...].astype(jnp.bfloat16)
    own_at = pl.multiple_of(position * block, block)
    for h in range(KVH):
        gathered[h, pl.ds(own_at, block), :] = own[h * block : (h + 1) * block, :]

    pl.semaphore_wait(barrier, len(peers))

    def remote(src, dst, send, recv, peer):
        return pltpu.make_async_remote_copy(
            src_ref=src,
            dst_ref=dst,
            send_sem=send,
            recv_sem=recv,
            device_id={"seq": peer},
            device_id_type=pl.DeviceIdType.MESH,
        )

    def rows_of(c, first, count):
        return gathered.at[
            pl.ds(c * HC, HC), pl.ds(pl.multiple_of(first * block, block), count * block)
        ]

    def gather_z(c, j):
        ref = rows_of(c, position, 1)
        return remote(ref, ref, gz_send.at[c, j - 1], gz_recv.at[c, j - 1], z_peer(j))

    def gather_z_in(c, j):
        ref = rows_of(c, core * (2 * planes) + y * planes + plane_before(j), 1)
        return remote(ref, ref, gz_send.at[c, j - 1], gz_recv.at[c, j - 1], z_peer(j))

    def gather_y(c, k):
        ref = rows_of(c, core * (2 * planes) + y * planes + plane_before(k), 1)
        return remote(ref, ref, gy_send.at[c, k], gy_recv.at[c, k], y_peer)

    def gather_y_in(c, k):
        ref = rows_of(c, core * (2 * planes) + (1 - y) * planes + plane_before(k), 1)
        return remote(ref, ref, gy_send.at[c, k], gy_recv.at[c, k], y_peer)

    def gather_core(c, which):
        yy = y if which == 0 else 1 - y
        ref = rows_of(c, core * (2 * planes) + yy * planes, planes)
        return remote(ref, ref, gc_send.at[c, which], gc_recv.at[c, which], core_peer)

    def gather_core_in(c, which):
        yy = y if which == 0 else 1 - y
        ref = rows_of(c, (1 - core) * (2 * planes) + yy * planes, planes)
        return remote(ref, ref, gc_send.at[c, which], gc_recv.at[c, which], core_peer)

    def core_copies(c):
        theirs = pl.ds((1 - core) * 2, 2)
        return (
            remote(part.at[c, theirs], core_in.at[c], rc_send.at[c, 0], rc_recv.at[c, 0], core_peer),
            remote(
                part_ml.at[c, theirs], core_in_ml.at[c], rc_send.at[c, 1], rc_recv.at[c, 1], core_peer
            ),
        )

    def y_copies(c):
        return (
            remote(yhalf.at[c, 1 - y], y_in.at[c], ry_send.at[c, 0], ry_recv.at[c, 0], y_peer),
            remote(yhalf_ml.at[c, 1 - y], y_in_ml.at[c], ry_send.at[c, 1], ry_recv.at[c, 1], y_peer),
        )

    def z_copies(c, j):
        theirs = pl.ds(pl.multiple_of(plane_at(j) * block, block), block)
        return (
            remote(
                zsend.at[c, :, theirs],
                z_in.at[c, j - 1],
                rz_send.at[c, j - 1, 0],
                rz_recv.at[c, j - 1, 0],
                z_peer(j),
            ),
            remote(
                zsend_ml.at[c],
                z_in_ml.at[c, j - 1],
                rz_send.at[c, j - 1, 1],
                rz_recv.at[c, j - 1, 1],
                z_peer(j),
            ),
        )

    for c in range(2):
        gather_y(c, 0).start()
        for j in range(1, planes):
            gather_z(c, j).start()

    lane = lax.broadcasted_iota(jnp.int32, (1, lanes), 1)
    lane_block = lax.div(lane, block)
    base_limit = jnp.zeros((1, lanes), jnp.int32)
    page_limits = [jnp.zeros((1, lanes), jnp.int32) for _ in range(pages_here)]
    for b in range(rows):
        at = (b % 2) * (2 * planes) + (b // 2 % 2) * planes + b // 4
        here = lane_block == at
        base_limit = jnp.where(here, offsets_ref[b] - me * base_len, base_limit)
        for p in range(pages_here):
            live = jnp.int32(0)
            for s in range(slots):
                live = live + jnp.where(
                    table_ref[s, b] == me * pages_here + p, lengths_ref[b] - s * page_len, 0
                )
            page_limits[p] = jnp.where(here, live, page_limits[p])
    new_limit = jnp.where(lane_block == position, lax.rem(lane, steps) + 1, 0)
    for i, limit in enumerate([base_limit] + page_limits + [new_limit]):
        limits[i : i + 1, :] = limit
    kv[new_at:, :] = jnp.concatenate(
        [new_ref[0].astype(jnp.float32), jnp.zeros((new_pad - steps, kv.shape[1]), jnp.float32)],
        axis=0,
    ).astype(jnp.bfloat16)

    key_blocks = [(0, base_len)]
    key_blocks += [(pages_at + p * page_len, page_len) for p in range(pages_here)]
    key_blocks += [(new_at, new_pad)]
    width = min(lanes, 512)
    per_width = width // quarter

    def forward_first(c):
        for j in range(1, planes):
            gather_z_in(c, j).wait_recv()
            gather_y(c, j).start()
            if c + 2 < CHUNKS:
                gather_z(c + 2, j).start()
        if c + 2 < CHUNKS:
            gather_y(c + 2, 0).start()
        gather_core(c, 0).start()

    def forward_second(c):
        for k in range(planes):
            gather_y_in(c, k).wait_recv()
        gather_core(c, 1).start()

    def attend(c):
        gather_core_in(c, 0).wait_recv()
        gather_core_in(c, 1).wait_recv()

        def lane_part(lb):
            start = pl.multiple_of(lb * width, width)
            tops, totals = [], []
            for hh in range(HC):
                h = c * HC + hh
                queries = gathered[h, pl.ds(start, width), :]
                keys = kv[:, 2 * h * HD : (2 * h + 1) * HD]
                values = kv[:, (2 * h + 1) * HD : (2 * h + 2) * HD]
                scores = lax.dot_general(
                    keys, queries, (((1,), (1,)), ((), ())), preferred_element_type=jnp.float32
                )
                pieces = []
                for i, (at, count) in enumerate(key_blocks):
                    key = lax.broadcasted_iota(jnp.int32, (count, width), 0)
                    limit = limits[i : i + 1, pl.ds(start, width)]
                    pieces.append(jnp.where(key < limit, scores[at : at + count], FAR))
                top = functools.reduce(
                    jnp.maximum, [jnp.max(x, axis=0, keepdims=True) for x in pieces]
                )
                weights = [jnp.exp2((x - top) * COEF) for x in pieces]
                total = sum(jnp.sum(x, axis=0, keepdims=True) for x in weights)
                rounded = jnp.concatenate([x.astype(jnp.bfloat16) for x in weights], axis=0)
                sums = lax.dot_general(
                    values, rounded, (((0,), (0,)), ((), ())), preferred_element_type=jnp.float32
                ).astype(jnp.bfloat16)
                for i in range(per_width):
                    part[c, lb * per_width + i, hh] = sums[:, i * quarter : (i + 1) * quarter]
                tops.append(top)
                totals.append(total)
            pad = [jnp.zeros((4 - HC, width), jnp.float32)] if HC < 4 else []
            both = jnp.concatenate(tops + pad + totals + pad, axis=0)
            for i in range(per_width):
                part_ml[c, lb * per_width + i] = both[:, i * quarter : (i + 1) * quarter]

        if lanes == width:
            lane_part(0)
        else:
            lax.fori_loop(0, lanes // width, lambda lb, _: (lane_part(lb), 0)[1], 0)
        for copy in core_copies(c):
            copy.start()

    def merge_ml(mine, theirs):
        top = jnp.maximum(mine[:4], theirs[:4])
        a = jnp.exp2((mine[:4] - top) * COEF)
        b = jnp.exp2((theirs[:4] - top) * COEF)
        return a, b, jnp.concatenate([top, a * mine[4:] + b * theirs[4:]], axis=0)

    def merge_core(c):
        for copy in core_copies(c):
            copy.wait_recv()
        for yy in range(2):
            a, b, ml = merge_ml(part_ml[c, core * 2 + yy], core_in_ml[c, yy])
            yhalf_ml[c, yy] = ml
            for hh in range(HC):
                merged = part[c, core * 2 + yy, hh].astype(jnp.float32) * a[hh : hh + 1]
                merged = merged + core_in[c, yy, hh].astype(jnp.float32) * b[hh : hh + 1]
                yhalf[c, yy, hh] = merged.astype(jnp.bfloat16)
        for copy in y_copies(c):
            copy.start()

    def merge_y(c):
        for copy in y_copies(c):
            copy.wait_recv()
        a, b, ml = merge_ml(yhalf_ml[c, y], y_in_ml[c])
        zsend_ml[c] = ml
        for hh in range(HC):
            merged = yhalf[c, y, hh].astype(jnp.float32) * a[hh : hh + 1]
            merged = merged + y_in[c, hh].astype(jnp.float32) * b[hh : hh + 1]
            zsend[c, hh] = merged.T.astype(jnp.bfloat16)
        for j in range(1, planes):
            for copy in z_copies(c, j):
                copy.start()

    def finish(c):
        for j in range(1, planes):
            for copy in z_copies(c, j):
                copy.wait_recv()
        parts = [zsend_ml[c]] + [z_in_ml[c, j - 1] for j in range(1, planes)]
        top = functools.reduce(jnp.maximum, [x[:4] for x in parts])
        scales = [jnp.exp2((x[:4] - top) * COEF) for x in parts]
        total = sum(s * x[4:] for s, x in zip(scales, parts))
        scales = [s / total if HC == 4 else s[:HC] / total[:HC] for s in scales]
        pad = [jnp.zeros((HD - planes * HC, quarter), jnp.float32)]
        factors[c] = jnp.concatenate(scales + pad, axis=0).T
        mine = pl.ds(pl.multiple_of(plane * block, block), block)
        by_source = factors[c, mine, :]
        for hh in range(HC):
            h = c * HC + hh
            result = zsend[c, hh, mine, :].astype(jnp.float32) * by_source[:, hh : hh + 1]
            for j in range(1, planes):
                at = j * HC + hh
                result = result + z_in[c, j - 1, hh].astype(jnp.float32) * by_source[:, at : at + 1]
            for g in range(GROUP):
                at = (h * GROUP + g) * HD
                out_ref[0, :, at : at + HD] = result[g * steps : (g + 1) * steps, :].astype(
                    jnp.bfloat16
                )

    stages = {
        "gather z": forward_first,
        "gather y": forward_second,
        "attend": attend,
        "core": merge_core,
        "y": merge_y,
        "z": finish,
    }
    loaded = False
    for stage, c in SCHEDULE:
        if stage == "attend" and not loaded:
            loaded = True
            for load in loads:
                load.wait()
        stages[stage](c)

    for c in range(CHUNKS):
        for j in range(1, planes):
            gather_z(c, j).wait_send()
            for copy in z_copies(c, j):
                copy.wait_send()
        for k in range(planes):
            gather_y(c, k).wait_send()
        gather_core(c, 0).wait_send()
        gather_core(c, 1).wait_send()
        for copy in core_copies(c) + y_copies(c):
            copy.wait_send()


def body(n, queries, base_cache, page_pool, new_cache, page_table, offsets, lengths):
    steps = queries.shape[1]
    block = GROUP * steps
    planes = n // 4
    quarter = planes * block
    lanes = n * block
    pages_here, page_len, columns = page_pool.shape
    keys = base_cache.shape[0] + pages_here * page_len + 16
    bf16, f32 = jnp.bfloat16, jnp.float32
    dma = pltpu.SemaphoreType.DMA
    smem = pl.BlockSpec(memory_space=pltpu.SMEM)
    vmem = pl.BlockSpec(memory_space=pltpu.VMEM)
    hbm = pl.BlockSpec(memory_space=pl.ANY)
    return pl.pallas_call(
        functools.partial(kernel, n),
        out_shape=jax.ShapeDtypeStruct(queries.shape, bf16),
        in_specs=[smem, smem, smem, vmem, vmem, hbm, hbm],
        out_specs=vmem,
        scratch_shapes=[
            pltpu.VMEM((keys, columns), bf16),
            pltpu.VMEM((max(8, pages_here + 2), lanes), jnp.int32),
            pltpu.VMEM((QH * steps, HD), f32),
            pltpu.VMEM((KVH, lanes, HD), bf16),
            pltpu.VMEM((CHUNKS, 4, HC, HD, quarter), bf16),
            pltpu.VMEM((CHUNKS, 4, 8, quarter), f32),
            pltpu.VMEM((CHUNKS, 2, HC, HD, quarter), bf16),
            pltpu.VMEM((CHUNKS, 2, 8, quarter), f32),
            pltpu.VMEM((CHUNKS, 2, HC, HD, quarter), bf16),
            pltpu.VMEM((CHUNKS, 2, 8, quarter), f32),
            pltpu.VMEM((CHUNKS, HC, HD, quarter), bf16),
            pltpu.VMEM((CHUNKS, 8, quarter), f32),
            pltpu.VMEM((CHUNKS, HC, quarter, HD), bf16),
            pltpu.VMEM((CHUNKS, 8, quarter), f32),
            pltpu.VMEM((CHUNKS, planes - 1, HC, block, HD), bf16),
            pltpu.VMEM((CHUNKS, planes - 1, 8, quarter), f32),
            pltpu.VMEM((CHUNKS, quarter, HD), f32),
            dma((1 + pages_here,)),
            dma((CHUNKS, planes - 1)),
            dma((CHUNKS, planes - 1)),
            dma((CHUNKS, planes)),
            dma((CHUNKS, planes)),
            dma((CHUNKS, 2)),
            dma((CHUNKS, 2)),
            dma((CHUNKS, 2)),
            dma((CHUNKS, 2)),
            dma((CHUNKS, 2)),
            dma((CHUNKS, 2)),
            dma((CHUNKS, planes - 1, 2)),
            dma((CHUNKS, planes - 1, 2)),
        ],
        compiler_params=pltpu.CompilerParams(
            collective_id=0, has_side_effects=True, vmem_limit_bytes=56 * 1024 * 1024
        ),
    )(page_table.T, offsets, lengths, queries, new_cache, base_cache, page_pool)


def solution(mesh):
    in_specs = (
        P(("groups", "seq"), None, None),
        P(("groups", "seq"), None),
        P(("groups", "seq"), None, None),
        P(("groups", "seq"), None, None),
        P("groups", None),
        P("groups"),
        P("groups"),
    )
    return jax.shard_map(
        functools.partial(body, mesh.shape["seq"]),
        mesh=mesh,
        in_specs=in_specs,
        out_specs=P(("groups", "seq"), None, None),
        check_vma=False,
    )
```
